32 devices in a mesh: tm: 4 (over y, x), rows: 8 (over z, core).
Axes of the slice: x: 2, y: 2, z: 4, core: 2. Of those that a mesh axis runs over, the one named last changes fastest.
Arguments:
- features: bfloat16 [16, 16, 64, 384], P('tm', 'rows'), may hold values from -6 to 6
- first_weight: bfloat16 [3, 3, 3, 384, 192], replicated, may hold values from -0.0625 to 0.0625
- first_bias: float32 [192], replicated, may hold values from -1.5 to 1.5
- first_gain: float32 [384], replicated, may hold values from 0.25 to 1.75
- second_weight: bfloat16 [3, 3, 3, 192, 192], replicated, may hold values from -0.078125 to 0.078125
- second_bias: float32 [192], replicated, may hold values from -1.5 to 1.5
- second_gain: float32 [192], replicated, may hold values from 0.25 to 1.75
- skip_weight: bfloat16 [384, 192], replicated, may hold values from -0.3125 to 0.3125
- skip_bias: float32 [192], replicated, may hold values from -1.5 to 1.5
Outputs:
- block_out: bfloat16 [16, 16, 64, 192], P('tm', 'rows')
The draws below stay inside these ranges and needn't reach their ends.
All inputs are finite; a program needn't handle non-finite values.
Results may differ from the reference program's by a relative error of at most 0.01.
Values may be sent and summed in bfloat16 or wider, within the bound.
A program may use at most 64 MiB of HBM per device.

```python
import jax
import jax.numpy as jnp
from jax import lax

C1 = 384
C2 = 192
W = 64
NT = 16
NH = 16


def block_levels(own_key, dims, pieces, least, largest):
    factor_of = 1.0
    for position, parts in pieces:
        steps = jax.random.uniform(jax.random.fold_in(jax.random.fold_in(own_key, 6), position), (parts,), jnp.float32, least / len(pieces), largest / len(pieces))
        factor_of = factor_of * jnp.repeat(jnp.exp(steps), dims[position] // parts).reshape((-1,) + (1,) * (len(dims) - 1 - position))
    return factor_of


def centred(key, dims, width, bound, cuts=(), kind=jnp.bfloat16):
    values = width * jax.random.normal(key, dims, jnp.float32)
    if cuts:
        values = values * block_levels(key, dims, cuts, -0.22, 0.18)
    return jnp.clip(values, -bound, bound).astype(kind)


def setup_inputs(seed: int = 0) -> dict:
    seeds = jax.random.split(jax.random.key(seed), 10)
    features = centred(seeds[0], (NT, NH, W, C1), 1.0, 6.0, ((0, 4), (1, 8)))
    first_weight = centred(seeds[1], (3, 3, 3, C1, C2), (27 * C1) ** -0.5, 0.0625)
    first_bias = centred(seeds[2], (C2,), 0.3, 1.5, (), jnp.float32)
    first_gain = jnp.clip(1.0 + 0.15 * jax.random.normal(seeds[3], (C1,), jnp.float32), 0.25, 1.75)
    second_weight = centred(seeds[4], (3, 3, 3, C2, C2), (27 * C2) ** -0.5, 0.078125)
    second_bias = centred(seeds[5], (C2,), 0.3, 1.5, (), jnp.float32)
    second_gain = jnp.clip(1.0 + 0.15 * jax.random.normal(seeds[6], (C2,), jnp.float32), 0.25, 1.75)
    skip_weight = centred(seeds[7], (C1, C2), C1 ** -0.5, 0.3125)
    skip_bias = centred(seeds[8], (C2,), 0.3, 1.5, (), jnp.float32)
    return {"features": features, "first_weight": first_weight, "first_bias": first_bias, "first_gain": first_gain, "second_weight": second_weight, "second_bias": second_bias, "second_gain": second_gain, "skip_weight": skip_weight, "skip_bias": skip_bias}


def activate(values, gain):
    floats = values.astype(jnp.float32)
    scaled = floats * lax.rsqrt(lax.optimization_barrier(jnp.mean(floats * floats, axis=-1, keepdims=True)) + 1e-06) * gain
    return jax.nn.silu(scaled).astype(jnp.bfloat16)

def convolve(padded, weight, bias):
    frames = padded.shape[0] - 2
    height = padded.shape[1] - 2
    across = padded.shape[2]
    channels = padded.shape[3]
    outputs = weight.shape[4]
    widened = jnp.pad(padded, ((0, 0), (0, 0), (1, 1), (0, 0)))
    summed = jnp.zeros((frames * height * across, outputs), jnp.float32)
    for time_tap in range(3):
        for row_tap in range(3):
            stacked = jnp.concatenate([widened[time_tap:time_tap + frames, row_tap:row_tap + height, col_tap:col_tap + across] for col_tap in range(3)], axis=-1)
            summed = summed + jnp.dot(stacked.reshape(-1, 3 * channels), weight[time_tap, row_tap].reshape(3 * channels, outputs), preferred_element_type=jnp.float32)
    return summed.reshape(frames, height, across, outputs) + bias

def reference(features, first_weight, first_bias, first_gain, second_weight, second_bias, second_gain, skip_weight, skip_bias):
    first_act = activate(features, first_gain)
    padded = jnp.pad(first_act, ((2, 0), (1, 1), (0, 0), (0, 0)))
    hidden = convolve(padded, first_weight, first_bias).astype(jnp.bfloat16)
    second_act = activate(hidden, second_gain)
    padded = jnp.pad(second_act, ((2, 0), (1, 1), (0, 0), (0, 0)))
    branch = convolve(padded, second_weight, second_bias)
    skipped = jnp.dot(features.reshape(-1, features.shape[-1]), skip_weight, preferred_element_type=jnp.float32)
    skipped = skipped.reshape(branch.shape)
    return (branch + skipped + skip_bias).astype(jnp.bfloat16)
```

```python
import functools

import jax
import jax.numpy as jnp
from jax import lax
from jax.experimental import pallas as pl
from jax.experimental.pallas import tpu as pltpu
from jax.sharding import PartitionSpec as P

MESH = pl.DeviceIdType.MESH
EDGE = 8


def activate(values, gain):
    floats = values.astype(jnp.float32)
    scaled = floats * lax.rsqrt(jnp.mean(floats * floats, axis=-1, keepdims=True) + 1e-06) * gain
    half = 0.5 * scaled
    return (half + half * jnp.tanh(half)).astype(jnp.bfloat16)


def times_rows(cells, weight):
    return lax.dot_general(
        cells, weight, (((1,), (1,)), ((), ())), preferred_element_type=jnp.float32
    )


def times(cells, weight):
    return jnp.dot(cells, weight, preferred_element_type=jnp.float32)


class Totals:
    def __init__(self, ref, across):
        self.ref, self.across, self.begun = ref, across, set()

    def clear_edges(self):
        shape = self.ref.shape
        zeros = jnp.zeros(shape[1:3] + (EDGE, shape[4]), jnp.float32)
        self.ref[0, :, :, 0:EDGE] = zeros
        self.ref[2, :, :, EDGE + self.across :] = zeros

    def add(self, tap, row, frame, value):
        for offset in range(value.shape[0]):
            key = (tap, row, frame + offset)
            place = (tap, row, frame + offset, pl.ds(EDGE, self.across))
            if key in self.begun:
                self.ref[place] += value[offset]
            else:
                self.begun.add(key)
                self.ref[place] = value[offset]

    def combined(self, row, frame):
        ref, across = self.ref, self.across
        return (
            ref[1, row, frame, pl.ds(EDGE, across)]
            + ref[0, row, frame, pl.ds(EDGE - 1, across)]
            + ref[2, row, frame, pl.ds(EDGE + 1, across)]
        )


def kernel(
    counts, x_hbm, w1_hbm, b1, g1, w2_hbm, b2, g2, ws_hbm, bs, out,
    x, w1, w2, ws, a1, a2, h1, h2, s1, s2, skip, p1, q1, p2, q2,
    load, row_send, row_recv, time_send, time_recv,
):
    ranks, bands = counts
    rank, band = lax.axis_index("tm"), lax.axis_index("rows")
    frames, _, across, inputs = x.shape
    outputs = out.shape[3]
    late = frames - 2
    has_up, has_down = band > 0, band < bands - 1
    has_before, has_after = rank > 0, rank < ranks - 1
    up = {"tm": rank, "rows": band - 1}
    down = {"tm": rank, "rows": band + 1}
    before = {"tm": rank - 1, "rows": band}
    after = {"tm": rank + 1, "rows": band}

    loads = [pltpu.make_async_copy(x_hbm, x, load.at[0])]
    for i in range(3):
        loads.append(pltpu.make_async_copy(w1_hbm.at[i], w1.at[i], load.at[1 + i]))
    loads.append(pltpu.make_async_copy(ws_hbm, ws, load.at[4]))
    loads.append(pltpu.make_async_copy(w2_hbm, w2, load.at[5]))
    for copy in loads:
        copy.start()

    barrier = pltpu.get_barrier_semaphore()
    for there, device in ((has_up, up), (has_down, down), (has_before, before), (has_after, after)):

        @pl.when(there)
        def _(device=device):
            pl.semaphore_signal(barrier, inc=1, device_id=device, device_id_type=MESH)

    @pl.when(jnp.logical_not(has_up))
    def _():
        h1[0] = jnp.zeros_like(h1[0])
        h2[0] = jnp.zeros_like(h2[0])

    @pl.when(jnp.logical_not(has_down))
    def _():
        h1[1] = jnp.zeros_like(h1[1])
        h2[1] = jnp.zeros_like(h2[1])

    @pl.when(jnp.logical_not(has_before))
    def _():
        q1[...] = jnp.zeros_like(q1)
        q2[...] = jnp.zeros_like(q2)

    t1, t2 = Totals(s1, across), Totals(s2, across)
    t1.clear_edges()
    t2.clear_edges()

    def row_copies(step, span):
        part = 2 * step + (1 if span[0] == 0 else 0)
        cut = pl.ds(span[0], span[1] - span[0])
        if step == 0:
            first, last = a1.at[cut, :, 0:inputs], a1.at[cut, :, inputs : 2 * inputs]
            halo = h1
        else:
            first, last, halo = a2.at[0, cut], a2.at[1, cut], h2
        upward = pltpu.make_async_remote_copy(
            first, halo.at[1, cut], row_send.at[part, 0], row_recv.at[part, 1],
            device_id=up, device_id_type=MESH,
        )
        downward = pltpu.make_async_remote_copy(
            last, halo.at[0, cut], row_send.at[part, 1], row_recv.at[part, 0],
            device_id=down, device_id_type=MESH,
        )
        return upward, downward

    def send_rows(step, span):
        upward, downward = row_copies(step, span)
        pl.when(has_up)(upward.start)
        pl.when(has_down)(downward.start)

    def receive_rows(step, span):
        upward, downward = row_copies(step, span)
        pl.when(has_down)(upward.wait_recv)
        pl.when(has_up)(downward.wait_recv)

    def time_copy(step):
        source, target = ((p1, q1), (p2, q2))[step]
        return pltpu.make_async_remote_copy(
            source, target, time_send.at[step], time_recv.at[step],
            device_id=after, device_id_type=MESH,
        )

    early_span, late_span = (0, late), (late, frames)

    def first_act(span):
        for f in range(*span):
            for r in range(2):
                a1[f, :, r * inputs : (r + 1) * inputs] = activate(x[f, r], g1[...])

    loads[0].wait()
    first_act(late_span)
    pl.semaphore_wait(
        barrier,
        has_up.astype(jnp.int32) + has_down.astype(jnp.int32)
        + has_before.astype(jnp.int32) + has_after.astype(jnp.int32),
    )
    send_rows(0, late_span)
    first_act(early_span)
    send_rows(0, early_span)

    def split(value, span):
        return value.reshape(span[1] - span[0], across, outputs)

    def local1(i, span):
        cells = a1[span[0] : span[1]].reshape(-1, 2 * inputs)
        for k in range(3):
            for r in range(2):
                weight = jnp.concatenate([w1[i, 1 - r, k], w1[i, 2 - r, k]], axis=-1)
                t1.add(k, r, span[0] + 2 - i, split(times_rows(cells, weight), span))

    def halo1(i, span):
        for r in range(2):
            cells = h1[r, span[0] : span[1]].reshape(-1, inputs)
            for k in range(3):
                t1.add(k, r, span[0] + 2 - i, split(times_rows(cells, w1[i, 2 * r, k]), span))

    def local2(i, span):
        top = a2[0, span[0] : span[1]].reshape(-1, outputs)
        low = a2[1, span[0] : span[1]].reshape(-1, outputs)
        for k in range(3):
            for r in range(2):
                value = times(top, w2[i, 1 - r, k]) + times(low, w2[i, 2 - r, k])
                t2.add(k, r, span[0] + 2 - i, split(value, span))

    def halo2(i, span):
        for r in range(2):
            cells = h2[r, span[0] : span[1]].reshape(-1, outputs)
            for k in range(3):
                t2.add(k, r, span[0] + 2 - i, split(times(cells, w2[i, 2 * r, k]), span))

    def send_time(step):
        total, source = ((t1, p1), (t2, p2))[step]
        for f in range(2):
            for r in range(2):
                source[f, r] = total.combined(r, frames + f).astype(jnp.bfloat16)
        pl.when(has_after)(time_copy(step).start)

    def second_act(span):
        for f in range(*span):
            for r in range(2):
                value = t1.combined(r, f) + b1[...]
                if f < 2:
                    value = value + q1[f, r].astype(jnp.float32)
                a2[r, f] = activate(value.astype(jnp.bfloat16), g2[...])

    def finish(span):
        for f in range(*span):
            for r in range(2):
                value = t2.combined(r, f) + skip[f, r] + (b2[...] + bs[...])
                if f < 2:
                    value = value + q2[f, r].astype(jnp.float32)
                out[f, r] = value.astype(out.dtype)

    whole = (0, frames)
    for i in range(2):
        loads[1 + i].wait()
        local1(i, whole)
    receive_rows(0, late_span)
    halo1(0, late_span)
    halo1(1, late_span)
    send_time(0)
    loads[3].wait()
    local1(2, whole)
    receive_rows(0, early_span)
    halo1(0, early_span)
    halo1(1, early_span)
    halo1(2, whole)
    second_act(late_span)
    send_rows(1, late_span)

    loads[5].wait()
    for i in range(3):
        local2(i, late_span)
    loads[4].wait()
    skip[...] = times_rows(x[...].reshape(-1, inputs), ws[...]).reshape(skip.shape)

    pl.when(has_before)(time_copy(0).wait_recv)
    second_act(early_span)
    send_rows(1, early_span)
    receive_rows(1, late_span)
    halo2(0, late_span)
    halo2(1, late_span)
    send_time(1)
    halo2(2, late_span)
    for i in range(3):
        local2(i, early_span)
    receive_rows(1, early_span)
    for i in range(3):
        halo2(i, early_span)
    finish(late_span)
    pl.when(has_before)(time_copy(1).wait_recv)
    finish(early_span)

    for step in range(2):
        pl.when(has_after)(time_copy(step).wait_send)
        for span in (late_span, early_span):
            upward, downward = row_copies(step, span)
            pl.when(has_up)(upward.wait_send)
            pl.when(has_down)(downward.wait_send)


def per_device(counts, features, w1, b1, g1, w2, b2, g2, ws, bs):
    frames, height, across, inputs = features.shape
    outputs = w1.shape[4]
    bf16, f32 = jnp.bfloat16, jnp.float32
    any_space = pl.BlockSpec(memory_space=pl.ANY)
    vmem = pl.BlockSpec(memory_space=pltpu.VMEM)
    totals = pltpu.VMEM((3, height, frames + 2, across + 2 * EDGE, outputs), f32)
    passed = pltpu.VMEM((2, height, across, outputs), bf16)
    return pl.pallas_call(
        functools.partial(kernel, counts),
        out_shape=jax.ShapeDtypeStruct((frames, height, across, outputs), bf16),
        in_specs=[any_space, any_space, vmem, vmem, any_space, vmem, vmem, any_space, vmem],
        out_specs=vmem,
        scratch_shapes=[
            pltpu.VMEM(features.shape, bf16),
            pltpu.VMEM((3, 3, 3, outputs, inputs), bf16),
            pltpu.VMEM((3, 3, 3, outputs, outputs), bf16),
            pltpu.VMEM((outputs, inputs), bf16),
            pltpu.VMEM((frames, across, 2 * inputs), bf16),
            pltpu.VMEM((2, frames, across, outputs), bf16),
            pltpu.VMEM((2, frames, across, inputs), bf16),
            pltpu.VMEM((2, frames, across, outputs), bf16),
            totals,
            totals,
            pltpu.VMEM((frames, height, across, outputs), f32),
            passed, passed, passed, passed,
            pltpu.SemaphoreType.DMA((6,)),
            pltpu.SemaphoreType.DMA((4, 2)),
            pltpu.SemaphoreType.DMA((4, 2)),
            pltpu.SemaphoreType.DMA((2,)),
            pltpu.SemaphoreType.DMA((2,)),
        ],
        compiler_params=pltpu.CompilerParams(
            collective_id=0, has_side_effects=True, vmem_limit_bytes=40 * 1024 * 1024
        ),
        name="block",
    )(
        features,
        jnp.swapaxes(w1, 3, 4),
        b1.reshape(1, -1),
        g1.reshape(1, -1),
        w2,
        b2.reshape(1, -1),
        g2.reshape(1, -1),
        jnp.swapaxes(ws, 0, 1),
        bs.reshape(1, -1),
    )


def solution(mesh):
    counts = (mesh.shape["tm"], mesh.shape["rows"])
    return jax.shard_map(
        functools.partial(per_device, counts),
        mesh=mesh,
        in_specs=(P("tm", "rows", None, None), P(), P(), P(), P(), P(), P(), P(), P()),
        out_specs=P("tm", "rows", None, None),
        check_vma=False,
    )
```

```python
import functools

import jax
import jax.numpy as jnp
from jax import lax
from jax.experimental import pallas as pl
from jax.experimental.pallas import tpu as pltpu
from jax.sharding import PartitionSpec as P

MESH = pl.DeviceIdType.MESH
EDGE = 8


def activate(values, gain):
    floats = values.astype(jnp.float32)
    scaled = floats * lax.rsqrt(jnp.mean(floats * floats, axis=-1, keepdims=True) + 1e-06) * gain
    half = 0.5 * scaled
    return (half + half * jnp.tanh(half)).astype(jnp.bfloat16)


def times_rows(cells, weight):
    return lax.dot_general(
        cells, weight, (((1,), (1,)), ((), ())), preferred_element_type=jnp.float32
    )


def times(cells, weight):
    return jnp.dot(cells, weight, preferred_element_type=jnp.float32)


class Totals:
    def __init__(self, ref, across):
        self.ref, self.across, self.begun = ref, across, set()

    def clear_edges(self):
        shape = self.ref.shape
        zeros = jnp.zeros(shape[1:3] + (EDGE, shape[4]), jnp.float32)
        self.ref[0, :, :, 0:EDGE] = zeros
        self.ref[2, :, :, EDGE + self.across :] = zeros

    def add(self, tap, row, frame, value):
        for offset in range(value.shape[0]):
            key = (tap, row, frame + offset)
            place = (tap, row, frame + offset, pl.ds(EDGE, self.across))
            if key in self.begun:
                self.ref[place] += value[offset]
            else:
                self.begun.add(key)
                self.ref[place] = value[offset]

    def combined(self, row, frame):
        ref, across = self.ref, self.across
        return (
            ref[1, row, frame, pl.ds(EDGE, across)]
            + ref[0, row, frame, pl.ds(EDGE - 1, across)]
            + ref[2, row, frame, pl.ds(EDGE + 1, across)]
        )


def kernel(
    counts, x_hbm, w1_hbm, b1_hbm, g1_hbm, w2_hbm, b2_hbm, g2_hbm, ws_hbm, bs_hbm, out,
    b1, g1, b2, g2, bs, x, w1, w2, ws, a1, a2, h1, h2, s1, s2, skip, p1, q1, p2, q2,
    load, row_send, row_recv, time_send, time_recv,
):
    ranks, bands = counts
    rank, band = lax.axis_index("tm"), lax.axis_index("rows")
    frames, _, across, inputs = x.shape
    outputs = out.shape[3]
    late = frames - 2
    has_up, has_down = band > 0, band < bands - 1
    has_before, has_after = rank > 0, rank < ranks - 1
    up = {"tm": rank, "rows": band - 1}
    down = {"tm": rank, "rows": band + 1}
    before = {"tm": rank - 1, "rows": band}
    after = {"tm": rank + 1, "rows": band}

    loads = [pltpu.make_async_copy(x_hbm, x, load.at[0])]
    for i in range(3):
        loads.append(pltpu.make_async_copy(w1_hbm.at[i], w1.at[i], load.at[1 + i]))
    loads.append(pltpu.make_async_copy(ws_hbm, ws, load.at[4]))
    loads.append(pltpu.make_async_copy(w2_hbm, w2, load.at[5]))
    vectors = ((g1_hbm, g1), (b1_hbm, b1), (g2_hbm, g2), (b2_hbm, b2), (bs_hbm, bs))
    for index, (source, target) in enumerate(vectors):
        loads.insert(1 + index, pltpu.make_async_copy(source, target, load.at[6 + index]))
    for copy in loads:
        copy.start()
    small, loads = loads[1:6], loads[:1] + loads[6:]

    barrier = pltpu.get_barrier_semaphore()
    for there, device in ((has_up, up), (has_down, down), (has_before, before), (has_after, after)):

        @pl.when(there)
        def _(device=device):
            pl.semaphore_signal(barrier, inc=1, device_id=device, device_id_type=MESH)

    @pl.when(jnp.logical_not(has_up))
    def _():
        h1[0] = jnp.zeros_like(h1[0])
        h2[0] = jnp.zeros_like(h2[0])

    @pl.when(jnp.logical_not(has_down))
    def _():
        h1[1] = jnp.zeros_like(h1[1])
        h2[1] = jnp.zeros_like(h2[1])

    @pl.when(jnp.logical_not(has_before))
    def _():
        q1[...] = jnp.zeros_like(q1)
        q2[...] = jnp.zeros_like(q2)

    t1, t2 = Totals(s1, across), Totals(s2, across)
    t1.clear_edges()
    t2.clear_edges()

    def row_copies(step, span):
        part = 2 * step + (1 if span[0] == 0 else 0)
        cut = pl.ds(span[0], span[1] - span[0])
        if step == 0:
            first, last = a1.at[cut, :, 0:inputs], a1.at[cut, :, inputs : 2 * inputs]
            halo = h1
        else:
            first, last, halo = a2.at[0, cut], a2.at[1, cut], h2
        upward = pltpu.make_async_remote_copy(
            first, halo.at[1, cut], row_send.at[part, 0], row_recv.at[part, 1],
            device_id=up, device_id_type=MESH,
        )
        downward = pltpu.make_async_remote_copy(
            last, halo.at[0, cut], row_send.at[part, 1], row_recv.at[part, 0],
            device_id=down, device_id_type=MESH,
        )
        return upward, downward

    def send_rows(step, span):
        upward, downward = row_copies(step, span)
        pl.when(has_up)(upward.start)
        pl.when(has_down)(downward.start)

    def receive_rows(step, span):
        upward, downward = row_copies(step, span)
        pl.when(has_down)(upward.wait_recv)
        pl.when(has_up)(downward.wait_recv)

    def time_copy(step):
        source, target = ((p1, q1), (p2, q2))[step]
        return pltpu.make_async_remote_copy(
            source, target, time_send.at[step], time_recv.at[step],
            device_id=after, device_id_type=MESH,
        )

    early_span, late_span = (0, late), (late, frames)

    def first_act(span):
        for f in range(*span):
            for r in range(2):
                a1[f, :, r * inputs : (r + 1) * inputs] = activate(x[f, r], g1[...].reshape(1, -1))

    loads[0].wait()
    for copy in small:
        copy.wait()
    first_act(late_span)
    pl.semaphore_wait(
        barrier,
        has_up.astype(jnp.int32) + has_down.astype(jnp.int32)
        + has_before.astype(jnp.int32) + has_after.astype(jnp.int32),
    )
    send_rows(0, late_span)
    first_act(early_span)
    send_rows(0, early_span)

    def split(value, span):
        return value.reshape(span[1] - span[0], across, outputs)

    def local1(i, span):
        cells = a1[span[0] : span[1]].reshape(-1, 2 * inputs)
        for k in range(3):
            for r in range(2):
                weight = jnp.concatenate([w1[i, 1 - r, k], w1[i, 2 - r, k]], axis=-1)
                t1.add(k, r, span[0] + 2 - i, split(times_rows(cells, weight), span))

    def halo1(i, span):
        for r in range(2):
            cells = h1[r, span[0] : span[1]].reshape(-1, inputs)
            for k in range(3):
                t1.add(k, r, span[0] + 2 - i, split(times_rows(cells, w1[i, 2 * r, k]), span))

    def local2(i, span):
        top = a2[0, span[0] : span[1]].reshape(-1, outputs)
        low = a2[1, span[0] : span[1]].reshape(-1, outputs)
        for k in range(3):
            for r in range(2):
                value = times(top, w2[i, 1 - r, k]) + times(low, w2[i, 2 - r, k])
                t2.add(k, r, span[0] + 2 - i, split(value, span))

    def halo2(i, span):
        for r in range(2):
            cells = h2[r, span[0] : span[1]].reshape(-1, outputs)
            for k in range(3):
                t2.add(k, r, span[0] + 2 - i, split(times(cells, w2[i, 2 * r, k]), span))

    def send_time(step):
        total, source = ((t1, p1), (t2, p2))[step]
        for f in range(2):
            for r in range(2):
                source[f, r] = total.combined(r, frames + f).astype(jnp.bfloat16)
        pl.when(has_after)(time_copy(step).start)

    def second_act(span):
        for f in range(*span):
            for r in range(2):
                value = t1.combined(r, f) + b1[...].reshape(1, -1)
                if f < 2:
                    value = value + q1[f, r].astype(jnp.float32)
                a2[r, f] = activate(value.astype(jnp.bfloat16), g2[...].reshape(1, -1))

    def finish(span):
        for f in range(*span):
            for r in range(2):
                value = t2.combined(r, f) + skip[f, r] + (b2[...].reshape(1, -1) + bs[...].reshape(1, -1))
                if f < 2:
                    value = value + q2[f, r].astype(jnp.float32)
                out[f, r] = value.astype(out.dtype)

    whole = (0, frames)
    for i in range(2):
        loads[1 + i].wait()
        local1(i, whole)
    receive_rows(0, late_span)
    halo1(0, late_span)
    halo1(1, late_span)
    send_time(0)
    loads[3].wait()
    local1(2, whole)
    receive_rows(0, early_span)
    halo1(0, early_span)
    halo1(1, early_span)
    halo1(2, whole)
    second_act(late_span)
    send_rows(1, late_span)

    loads[5].wait()
    for i in range(2):
        local2(i, late_span)
    loads[4].wait()
    skip[...] = times_rows(x[...].reshape(-1, inputs), ws[...]).reshape(skip.shape)

    pl.when(has_before)(time_copy(0).wait_recv)
    second_act(early_span)
    send_rows(1, early_span)
    receive_rows(1, late_span)
    halo2(0, late_span)
    halo2(1, late_span)
    send_time(1)
    local2(2, whole)
    for i in range(2):
        local2(i, early_span)
    receive_rows(1, early_span)
    halo2(2, whole)
    for i in range(2):
        halo2(i, early_span)
    finish(late_span)
    pl.when(has_before)(time_copy(1).wait_recv)
    finish(early_span)

    for step in range(2):
        pl.when(has_after)(time_copy(step).wait_send)
        for span in (late_span, early_span):
            upward, downward = row_copies(step, span)
            pl.when(has_up)(upward.wait_send)
            pl.when(has_down)(downward.wait_send)


def per_device(counts, features, w1, b1, g1, w2, b2, g2, ws, bs):
    frames, height, across, inputs = features.shape
    outputs = w1.shape[4]
    bf16, f32 = jnp.bfloat16, jnp.float32
    hbm = pl.BlockSpec(memory_space=pltpu.HBM)
    vmem = pl.BlockSpec(memory_space=pltpu.VMEM)
    totals = pltpu.VMEM((3, height, frames + 2, across + 2 * EDGE, outputs), f32)
    passed = pltpu.VMEM((2, height, across, outputs), bf16)
    return pl.pallas_call(
        functools.partial(kernel, counts),
        out_shape=jax.ShapeDtypeStruct((frames, height, across, outputs), bf16),
        in_specs=[hbm] * 9,
        out_specs=vmem,
        scratch_shapes=[
            pltpu.VMEM(b1.shape, f32),
            pltpu.VMEM(g1.shape, f32),
            pltpu.VMEM(b2.shape, f32),
            pltpu.VMEM(g2.shape, f32),
            pltpu.VMEM(bs.shape, f32),
            pltpu.VMEM(features.shape, bf16),
            pltpu.VMEM((3, 3, 3, outputs, inputs), bf16),
            pltpu.VMEM((3, 3, 3, outputs, outputs), bf16),
            pltpu.VMEM((outputs, inputs), bf16),
            pltpu.VMEM((frames, across, 2 * inputs), bf16),
            pltpu.VMEM((2, frames, across, outputs), bf16),
            pltpu.VMEM((2, frames, across, inputs), bf16),
            pltpu.VMEM((2, frames, across, outputs), bf16),
            totals,
            totals,
            pltpu.VMEM((frames, height, across, outputs), f32),
            passed, passed, passed, passed,
            pltpu.SemaphoreType.DMA((11,)),
            pltpu.SemaphoreType.DMA((4, 2)),
            pltpu.SemaphoreType.DMA((4, 2)),
            pltpu.SemaphoreType.DMA((2,)),
            pltpu.SemaphoreType.DMA((2,)),
        ],
        compiler_params=pltpu.CompilerParams(
            collective_id=0, has_side_effects=True, vmem_limit_bytes=64 * 1024 * 1024
        ),
        name="block",
    )(
        features,
        jnp.swapaxes(w1, 3, 4),
        b1,
        g1,
        w2,
        b2,
        g2,
        jnp.swapaxes(ws, 0, 1),
        bs,
    )


def solution(mesh):
    counts = (mesh.shape["tm"], mesh.shape["rows"])
    return jax.shard_map(
        functools.partial(per_device, counts),
        mesh=mesh,
        in_specs=(P("tm", "rows", None, None), P(), P(), P(), P(), P(), P(), P(), P()),
        out_specs=P("tm", "rows", None, None),
        check_vma=False,
    )
```

```python
import functools

import jax
import jax.numpy as jnp
from jax import lax
from jax.experimental import pallas as pl
from jax.experimental.pallas import tpu as pltpu
from jax.sharding import PartitionSpec as P

MESH = pl.DeviceIdType.MESH
EDGE = 8


def activate(values, gain):
    floats = values.astype(jnp.float32)
    scaled = floats * lax.rsqrt(jnp.mean(floats * floats, axis=-1, keepdims=True) + 1e-06) * gain
    half = 0.5 * scaled
    return (half + half * jnp.tanh(half)).astype(jnp.bfloat16)


def times_rows(cells, weight):
    return lax.dot_general(
        cells, weight, (((1,), (1,)), ((), ())), preferred_element_type=jnp.float32
    )


def times(cells, weight):
    return jnp.dot(cells, weight, preferred_element_type=jnp.float32)


class Totals:
    def __init__(self, ref, across):
        self.ref, self.across, self.begun = ref, across, set()

    def clear_edges(self):
        shape = self.ref.shape
        zeros = jnp.zeros(shape[1:3] + (EDGE, shape[4]), jnp.float32)
        self.ref[0, :, :, 0:EDGE] = zeros
        self.ref[2, :, :, EDGE + self.across :] = zeros

    def add(self, tap, row, frame, value):
        for offset in range(value.shape[0]):
            key = (tap, row, frame + offset)
            place = (tap, row, frame + offset, pl.ds(EDGE, self.across))
            if key in self.begun:
                self.ref[place] += value[offset]
            else:
                self.begun.add(key)
                self.ref[place] = value[offset]

    def combined(self, row, frame):
        ref, across = self.ref, self.across
        return (
            ref[1, row, frame, pl.ds(EDGE, across)]
            + ref[0, row, frame, pl.ds(EDGE - 1, across)]
            + ref[2, row, frame, pl.ds(EDGE + 1, across)]
        )


def kernel(
    counts, x_hbm, w1_hbm, b1_hbm, g1_hbm, w2_hbm, b2_hbm, g2_hbm, ws_hbm, bs_hbm, out,
    b1, g1, b2, g2, bs, x, w1, w2, ws, a1, a2, h1, h2, s1, s2, skip, p1, q1, p2, q2,
    load, row_send, row_recv, time_send, time_recv,
):
    ranks, bands = counts
    rank, band = lax.axis_index("tm"), lax.axis_index("rows")
    frames, _, across, inputs = x.shape
    outputs = out.shape[3]
    late = frames - 2
    has_up, has_down = band > 0, band < bands - 1
    has_before, has_after = rank > 0, rank < ranks - 1
    up = {"tm": rank, "rows": band - 1}
    down = {"tm": rank, "rows": band + 1}
    before = {"tm": rank - 1, "rows": band}
    after = {"tm": rank + 1, "rows": band}

    loads = [pltpu.make_async_copy(x_hbm, x, load.at[0])]
    for i in range(3):
        loads.append(pltpu.make_async_copy(w1_hbm.at[i], w1.at[i], load.at[1 + i]))
    loads.append(pltpu.make_async_copy(ws_hbm, ws, load.at[4]))
    loads.append(pltpu.make_async_copy(w2_hbm, w2, load.at[5]))
    vectors = ((g1_hbm, g1), (b1_hbm, b1), (g2_hbm, g2), (b2_hbm, b2), (bs_hbm, bs))
    for index, (source, target) in enumerate(vectors):
        loads.insert(1 + index, pltpu.make_async_copy(source, target, load.at[6 + index]))
    for copy in loads:
        copy.start()
    small, loads = loads[1:6], loads[:1] + loads[6:]

    barrier = pltpu.get_barrier_semaphore()
    for there, device in ((has_up, up), (has_down, down), (has_before, before), (has_after, after)):

        @pl.when(there)
        def _(device=device):
            pl.semaphore_signal(barrier, inc=1, device_id=device, device_id_type=MESH)

    @pl.when(jnp.logical_not(has_up))
    def _():
        h1[0] = jnp.zeros_like(h1[0])
        h2[0] = jnp.zeros_like(h2[0])

    @pl.when(jnp.logical_not(has_down))
    def _():
        h1[1] = jnp.zeros_like(h1[1])
        h2[1] = jnp.zeros_like(h2[1])

    @pl.when(jnp.logical_not(has_before))
    def _():
        q1[...] = jnp.zeros_like(q1)
        q2[...] = jnp.zeros_like(q2)

    t2 = Totals(s2, across)
    t2.clear_edges()

    def row_copies(step, span):
        part = 2 * step + (1 if span[0] == 0 else 0)
        cut = pl.ds(span[0], span[1] - span[0])
        if step == 0:
            first, last = a1.at[cut, :, 0:inputs], a1.at[cut, :, inputs : 2 * inputs]
            halo = h1
        else:
            first, last, halo = a2.at[0, cut], a2.at[1, cut], h2
        upward = pltpu.make_async_remote_copy(
            first, halo.at[1, cut], row_send.at[part, 0], row_recv.at[part, 1],
            device_id=up, device_id_type=MESH,
        )
        downward = pltpu.make_async_remote_copy(
            last, halo.at[0, cut], row_send.at[part, 1], row_recv.at[part, 0],
            device_id=down, device_id_type=MESH,
        )
        return upward, downward

    def send_rows(step, span):
        upward, downward = row_copies(step, span)
        pl.when(has_up)(upward.start)
        pl.when(has_down)(downward.start)

    def receive_rows(step, span):
        upward, downward = row_copies(step, span)
        pl.when(has_down)(upward.wait_recv)
        pl.when(has_up)(downward.wait_recv)

    def time_copy(step):
        source, target = ((p1, q1), (p2, q2))[step]
        return pltpu.make_async_remote_copy(
            source, target, time_send.at[step], time_recv.at[step],
            device_id=after, device_id_type=MESH,
        )

    early_span, late_span = (0, late), (late, frames)

    def first_act(span):
        for f in range(*span):
            for r in range(2):
                a1[f, :, r * inputs : (r + 1) * inputs] = activate(x[f, r], g1[...].reshape(1, -1))

    loads[0].wait()
    for copy in small:
        copy.wait()
    first_act(late_span)
    pl.semaphore_wait(
        barrier,
        has_up.astype(jnp.int32) + has_down.astype(jnp.int32)
        + has_before.astype(jnp.int32) + has_after.astype(jnp.int32),
    )
    send_rows(0, late_span)
    first_act(early_span)
    send_rows(0, early_span)

    def split(value, span):
        return value.reshape(span[1] - span[0], across, outputs)

    lane = lax.broadcasted_iota(jnp.int32, (1, 2 * across), 1)
    column = lax.rem(lane, across)
    pair = 2 * across

    def local1(i):
        cells = a1[...].reshape(-1, 2 * inputs)
        for r in range(2):
            weight = jnp.concatenate([w1[i, 1 - r], w1[i, 2 - r]], axis=-1)
            value = times_rows(weight.reshape(-1, 2 * inputs), cells)
            s1[r, i] = value.reshape(3, outputs, -1)

    def halo1(i):
        for r in range(2):
            cells = h1[r].reshape(-1, inputs)
            value = times_rows(w1[i, 2 * r].reshape(-1, inputs), cells)
            s1[r, i] += value.reshape(3, outputs, -1)

    def turned(r, k, half):
        return pltpu.roll(s1[r, 1, k, :, half * pair : (half + 1) * pair], across, 1)

    def first_sum(r, group):
        taps = []
        for k in range(3):
            if group == 0:
                total = s1[r, 2, k, :, 0:pair] + jnp.where(lane >= across, turned(r, k, 0), 0.0)
            elif group == 1:
                total = s1[r, 2, k, :, pair:] + s1[r, 0, k, :, 0:pair]
                total += jnp.where(lane < across, turned(r, k, 0), turned(r, k, 1))
            else:
                total = s1[r, 0, k, :, pair:] + jnp.where(lane < across, turned(r, k, 1), 0.0)
            taps.append(total)
        from_left = jnp.where(column > 0, pltpu.roll(taps[0], 1, 1), 0.0)
        from_right = jnp.where(column < across - 1, pltpu.roll(taps[2], pair - 1, 1), 0.0)
        return taps[1] + from_left + from_right

    def local2(i, span):
        top = a2[0, span[0] : span[1]].reshape(-1, outputs)
        low = a2[1, span[0] : span[1]].reshape(-1, outputs)
        for k in range(3):
            for r in range(2):
                value = times(top, w2[i, 1 - r, k]) + times(low, w2[i, 2 - r, k])
                t2.add(k, r, span[0] + 2 - i, split(value, span))

    def halo2(i, span):
        for r in range(2):
            cells = h2[r, span[0] : span[1]].reshape(-1, outputs)
            for k in range(3):
                t2.add(k, r, span[0] + 2 - i, split(times(cells, w2[i, 2 * r, k]), span))

    def send_time(step):
        for r in range(2):
            if step == 0:
                p1[r] = first_sum(r, 2).astype(jnp.bfloat16)
            else:
                for f in range(2):
                    p2[f, r] = t2.combined(r, frames + f).astype(jnp.bfloat16)
        pl.when(has_after)(time_copy(step).start)

    def second_act(group):
        for r in range(2):
            value = first_sum(r, group)
            if group == 0:
                value = value + q1[r].astype(jnp.float32)
            spare = jnp.zeros((-outputs % 128, pair), jnp.float32)
            value = jnp.concatenate([value, spare], axis=0).T[:, :outputs]
            value = value + b1[...].reshape(1, -1)
            act = activate(value.astype(jnp.bfloat16), g2[...].reshape(1, -1))
            a2[r, 2 * group : 2 * group + 2] = act.reshape(2, across, outputs)

    def finish(span):
        for f in range(*span):
            for r in range(2):
                value = t2.combined(r, f) + skip[f, r] + (b2[...].reshape(1, -1) + bs[...].reshape(1, -1))
                if f < 2:
                    value = value + q2[f, r].astype(jnp.float32)
                out[f, r] = value.astype(out.dtype)

    whole = (0, frames)
    for i in range(2):
        loads[1 + i].wait()
        local1(i)
    receive_rows(0, late_span)
    receive_rows(0, early_span)
    halo1(0)
    halo1(1)
    send_time(0)
    loads[3].wait()
    local1(2)
    halo1(2)
    second_act(1)
    send_rows(1, late_span)

    loads[5].wait()
    for i in range(2):
        local2(i, late_span)
    loads[4].wait()
    skip[...] = times_rows(x[...].reshape(-1, inputs), ws[...]).reshape(skip.shape)

    pl.when(has_before)(time_copy(0).wait_recv)
    second_act(0)
    send_rows(1, early_span)
    receive_rows(1, late_span)
    halo2(0, late_span)
    halo2(1, late_span)
    send_time(1)
    local2(2, whole)
    for i in range(2):
        local2(i, early_span)
    receive_rows(1, early_span)
    halo2(2, whole)
    for i in range(2):
        halo2(i, early_span)
    finish(late_span)
    pl.when(has_before)(time_copy(1).wait_recv)
    finish(early_span)

    for step in range(2):
        pl.when(has_after)(time_copy(step).wait_send)
        for span in (late_span, early_span):
            upward, downward = row_copies(step, span)
            pl.when(has_up)(upward.wait_send)
            pl.when(has_down)(downward.wait_send)


def per_device(counts, features, w1, b1, g1, w2, b2, g2, ws, bs):
    frames, height, across, inputs = features.shape
    outputs = w1.shape[4]
    bf16, f32 = jnp.bfloat16, jnp.float32
    hbm = pl.BlockSpec(memory_space=pltpu.HBM)
    vmem = pl.BlockSpec(memory_space=pltpu.VMEM)
    totals = pltpu.VMEM((3, height, frames + 2, across + 2 * EDGE, outputs), f32)
    passed = pltpu.VMEM((2, height, across, outputs), bf16)
    turned = pltpu.VMEM((height, outputs, 2 * across), bf16)
    return pl.pallas_call(
        functools.partial(kernel, counts),
        out_shape=jax.ShapeDtypeStruct((frames, height, across, outputs), bf16),
        in_specs=[hbm] * 9,
        out_specs=vmem,
        scratch_shapes=[
            pltpu.VMEM(b1.shape, f32),
            pltpu.VMEM(g1.shape, f32),
            pltpu.VMEM(b2.shape, f32),
            pltpu.VMEM(g2.shape, f32),
            pltpu.VMEM(bs.shape, f32),
            pltpu.VMEM(features.shape, bf16),
            pltpu.VMEM((3, 3, 3, outputs, inputs), bf16),
            pltpu.VMEM((3, 3, 3, outputs, outputs), bf16),
            pltpu.VMEM((outputs, inputs), bf16),
            pltpu.VMEM((frames, across, 2 * inputs), bf16),
            pltpu.VMEM((2, frames, across, outputs), bf16),
            pltpu.VMEM((2, frames, across, inputs), bf16),
            pltpu.VMEM((2, frames, across, outputs), bf16),
            pltpu.VMEM((height, 3, 3, outputs, frames * across), f32),
            totals,
            pltpu.VMEM((frames, height, across, outputs), f32),
            turned, turned, passed, passed,
            pltpu.SemaphoreType.DMA((11,)),
            pltpu.SemaphoreType.DMA((4, 2)),
            pltpu.SemaphoreType.DMA((4, 2)),
            pltpu.SemaphoreType.DMA((2,)),
            pltpu.SemaphoreType.DMA((2,)),
        ],
        compiler_params=pltpu.CompilerParams(
            collective_id=0, has_side_effects=True, vmem_limit_bytes=64 * 1024 * 1024
        ),
        name="block",
    )(
        features,
        jnp.swapaxes(w1, 3, 4),
        b1,
        g1,
        w2,
        b2,
        g2,
        jnp.swapaxes(ws, 0, 1),
        bs,
    )


def solution(mesh):
    counts = (mesh.shape["tm"], mesh.shape["rows"])
    return jax.shard_map(
        functools.partial(per_device, counts),
        mesh=mesh,
        in_specs=(P("tm", "rows", None, None), P(), P(), P(), P(), P(), P(), P(), P()),
        out_specs=P("tm", "rows", None, None),
        check_vma=False,
    )
```

```python
import functools

import jax
import jax.numpy as jnp
from jax import lax
from jax.experimental import pallas as pl
from jax.experimental.pallas import tpu as pltpu
from jax.sharding import PartitionSpec as P

MESH = pl.DeviceIdType.MESH
EDGE = 8


def activate(values, gain):
    floats = values.astype(jnp.float32)
    scaled = floats * lax.rsqrt(jnp.mean(floats * floats, axis=-1, keepdims=True) + 1e-06) * gain
    half = 0.5 * scaled
    return (half + half * jnp.tanh(half)).astype(jnp.bfloat16)


def times_rows(cells, weight):
    return lax.dot_general(
        cells, weight, (((1,), (1,)), ((), ())), preferred_element_type=jnp.float32
    )


def times(cells, weight):
    return jnp.dot(cells, weight, preferred_element_type=jnp.float32)


class Totals:
    def __init__(self, ref, across):
        self.ref, self.across, self.begun = ref, across, set()

    def clear_edges(self):
        shape = self.ref.shape
        zeros = jnp.zeros(shape[1:3] + (EDGE, shape[4]), jnp.float32)
        self.ref[0, :, :, 0:EDGE] = zeros
        self.ref[2, :, :, EDGE + self.across :] = zeros

    def add(self, tap, row, frame, value):
        for offset in range(value.shape[0]):
            key = (tap, row, frame + offset)
            place = (tap, row, frame + offset, pl.ds(EDGE, self.across))
            if key in self.begun:
                self.ref[place] += value[offset]
            else:
                self.begun.add(key)
                self.ref[place] = value[offset]

    def combined(self, row, frame):
        ref, across = self.ref, self.across
        return (
            ref[1, row, frame, pl.ds(EDGE, across)]
            + ref[0, row, frame, pl.ds(EDGE - 1, across)]
            + ref[2, row, frame, pl.ds(EDGE + 1, across)]
        )


def kernel(
    counts, x_hbm, w1_hbm, b1_hbm, g1_hbm, w2_hbm, b2_hbm, g2_hbm, ws_hbm, bs_hbm, out,
    b1, g1, b2, g2, bs, x, w1, w2, ws, a1, a2, h1, h2, s1, s2, skip, p1, q1, p2, q2,
    load, row_send, row_recv, time_send, time_recv,
):
    ranks, bands = counts
    rank, band = lax.axis_index("tm"), lax.axis_index("rows")
    frames, _, across, inputs = x.shape
    outputs = out.shape[3]
    late = frames - 2
    has_up, has_down = band > 0, band < bands - 1
    has_before, has_after = rank > 0, rank < ranks - 1
    up = {"tm": rank, "rows": band - 1}
    down = {"tm": rank, "rows": band + 1}
    before = {"tm": rank - 1, "rows": band}
    after = {"tm": rank + 1, "rows": band}

    loads = [pltpu.make_async_copy(x_hbm, x, load.at[0])]
    for i in range(3):
        loads.append(pltpu.make_async_copy(w1_hbm.at[i], w1.at[i], load.at[1 + i]))
    loads.append(pltpu.make_async_copy(ws_hbm, ws, load.at[4]))
    loads.append(pltpu.make_async_copy(w2_hbm, w2, load.at[5]))
    vectors = ((g1_hbm, g1), (b1_hbm, b1), (g2_hbm, g2), (b2_hbm, b2), (bs_hbm, bs))
    for index, (source, target) in enumerate(vectors):
        loads.insert(1 + index, pltpu.make_async_copy(source, target, load.at[6 + index]))
    for copy in loads:
        copy.start()
    small, loads = loads[1:6], loads[:1] + loads[6:]

    barrier = pltpu.get_barrier_semaphore()
    for there, device in ((has_up, up), (has_down, down), (has_before, before), (has_after, after)):

        @pl.when(there)
        def _(device=device):
            pl.semaphore_signal(barrier, inc=1, device_id=device, device_id_type=MESH)

    @pl.when(jnp.logical_not(has_up))
    def _():
        h1[0] = jnp.zeros_like(h1[0])
        h2[0] = jnp.zeros_like(h2[0])

    @pl.when(jnp.logical_not(has_down))
    def _():
        h1[1] = jnp.zeros_like(h1[1])
        h2[1] = jnp.zeros_like(h2[1])

    @pl.when(jnp.logical_not(has_before))
    def _():
        q1[...] = jnp.zeros_like(q1)
        q2[...] = jnp.zeros_like(q2)

    t2 = Totals(s2, across)
    t2.clear_edges()

    def row_copies(step, span):
        part = 2 * step + (1 if span[0] == 0 else 0)
        cut = pl.ds(span[0], span[1] - span[0])
        if step == 0:
            first, last = a1.at[cut, :, 0:inputs], a1.at[cut, :, inputs : 2 * inputs]
            halo = h1
        else:
            first, last, halo = a2.at[0, cut], a2.at[1, cut], h2
        upward = pltpu.make_async_remote_copy(
            first, halo.at[1, cut], row_send.at[part, 0], row_recv.at[part, 1],
            device_id=up, device_id_type=MESH,
        )
        downward = pltpu.make_async_remote_copy(
            last, halo.at[0, cut], row_send.at[part, 1], row_recv.at[part, 0],
            device_id=down, device_id_type=MESH,
        )
        return upward, downward

    def send_rows(step, span):
        upward, downward = row_copies(step, span)
        pl.when(has_up)(upward.start)
        pl.when(has_down)(downward.start)

    def receive_rows(step, span):
        upward, downward = row_copies(step, span)
        pl.when(has_down)(upward.wait_recv)
        pl.when(has_up)(downward.wait_recv)

    def time_copy(step):
        source, target = ((p1, q1), (p2, q2))[step]
        return pltpu.make_async_remote_copy(
            source, target, time_send.at[step], time_recv.at[step],
            device_id=after, device_id_type=MESH,
        )

    early_span, late_span = (0, late), (late, frames)

    def first_act(span):
        for f in range(*span):
            for r in range(2):
                a1[f, :, r * inputs : (r + 1) * inputs] = activate(x[f, r], g1[...].reshape(1, -1))

    loads[0].wait()
    for copy in small:
        copy.wait()
    first_act(late_span)
    pl.semaphore_wait(
        barrier,
        has_up.astype(jnp.int32) + has_down.astype(jnp.int32)
        + has_before.astype(jnp.int32) + has_after.astype(jnp.int32),
    )
    send_rows(0, late_span)
    first_act(early_span)
    send_rows(0, early_span)

    def split(value, span):
        return value.reshape(span[1] - span[0], across, outputs)

    lane = lax.broadcasted_iota(jnp.int32, (1, 2 * across), 1)
    column = lax.rem(lane, across)
    pair = 2 * across

    def local1(i):
        cells = a1[...].reshape(-1, 2 * inputs)
        for r in range(2):
            weight = jnp.concatenate([w1[i, 1 - r], w1[i, 2 - r]], axis=-1)
            value = times_rows(weight.reshape(-1, 2 * inputs), cells)
            s1[r, i] = value.reshape(3, outputs, -1)

    def halo1(i, span):
        cut = slice(span[0] * across, span[1] * across)
        for r in range(2):
            cells = h1[r, span[0] : span[1]].reshape(-1, inputs)
            value = times_rows(w1[i, 2 * r].reshape(-1, inputs), cells)
            s1[r, i, :, :, cut] += value.reshape(3, outputs, -1)

    def turned(r, k, half):
        return pltpu.roll(s1[r, 1, k, :, half * pair : (half + 1) * pair], across, 1)

    def first_sum(r, group):
        taps = []
        for k in range(3):
            if group == 0:
                total = s1[r, 2, k, :, 0:pair] + jnp.where(lane >= across, turned(r, k, 0), 0.0)
            elif group == 1:
                total = s1[r, 2, k, :, pair:] + s1[r, 0, k, :, 0:pair]
                total += jnp.where(lane < across, turned(r, k, 0), turned(r, k, 1))
            else:
                total = s1[r, 0, k, :, pair:] + jnp.where(lane < across, turned(r, k, 1), 0.0)
            taps.append(total)
        from_left = jnp.where(column > 0, pltpu.roll(taps[0], 1, 1), 0.0)
        from_right = jnp.where(column < across - 1, pltpu.roll(taps[2], pair - 1, 1), 0.0)
        return taps[1] + from_left + from_right

    def local2(i, span):
        top = a2[0, span[0] : span[1]].reshape(-1, outputs)
        low = a2[1, span[0] : span[1]].reshape(-1, outputs)
        for k in range(3):
            for r in range(2):
                value = times(top, w2[i, 1 - r, k]) + times(low, w2[i, 2 - r, k])
                t2.add(k, r, span[0] + 2 - i, split(value, span))

    def halo2(i, span):
        for r in range(2):
            cells = h2[r, span[0] : span[1]].reshape(-1, outputs)
            for k in range(3):
                t2.add(k, r, span[0] + 2 - i, split(times(cells, w2[i, 2 * r, k]), span))

    def send_time(step):
        for r in range(2):
            if step == 0:
                p1[r] = first_sum(r, 2).astype(jnp.bfloat16)
            else:
                for f in range(2):
                    p2[f, r] = t2.combined(r, frames + f).astype(jnp.bfloat16)
        pl.when(has_after)(time_copy(step).start)

    def second_act(group):
        for r in range(2):
            value = first_sum(r, group)
            if group == 0:
                value = value + q1[r].astype(jnp.float32)
            spare = jnp.zeros((-outputs % 128, pair), jnp.float32)
            value = jnp.concatenate([value, spare], axis=0).T[:, :outputs]
            value = value + b1[...].reshape(1, -1)
            act = activate(value.astype(jnp.bfloat16), g2[...].reshape(1, -1))
            a2[r, 2 * group : 2 * group + 2] = act.reshape(2, across, outputs)

    def finish(span):
        for f in range(*span):
            for r in range(2):
                value = t2.combined(r, f) + skip[f, r] + (b2[...].reshape(1, -1) + bs[...].reshape(1, -1))
                if f < 2:
                    value = value + q2[f, r].astype(jnp.float32)
                out[f, r] = value.astype(out.dtype)

    whole = (0, frames)
    for i in range(2):
        loads[1 + i].wait()
        local1(i)
    receive_rows(0, late_span)
    halo1(0, late_span)
    halo1(1, late_span)
    send_time(0)
    loads[3].wait()
    local1(2)
    receive_rows(0, early_span)
    halo1(0, early_span)
    halo1(1, early_span)
    halo1(2, whole)
    second_act(1)
    send_rows(1, late_span)

    loads[5].wait()
    for i in range(2):
        local2(i, late_span)
    loads[4].wait()
    skip[...] = times_rows(x[...].reshape(-1, inputs), ws[...]).reshape(skip.shape)

    receive_rows(1, late_span)
    halo2(0, late_span)
    halo2(1, late_span)
    send_time(1)
    pl.when(has_before)(time_copy(0).wait_recv)
    second_act(0)
    send_rows(1, early_span)
    local2(2, whole)
    for i in range(2):
        local2(i, early_span)
    receive_rows(1, early_span)
    halo2(2, whole)
    for i in range(2):
        halo2(i, early_span)
    finish(late_span)
    pl.when(has_before)(time_copy(1).wait_recv)
    finish(early_span)

    for step in range(2):
        pl.when(has_after)(time_copy(step).wait_send)
        for span in (late_span, early_span):
            upward, downward = row_copies(step, span)
            pl.when(has_up)(upward.wait_send)
            pl.when(has_down)(downward.wait_send)


def per_device(counts, features, w1, b1, g1, w2, b2, g2, ws, bs):
    frames, height, across, inputs = features.shape
    outputs = w1.shape[4]
    bf16, f32 = jnp.bfloat16, jnp.float32
    hbm = pl.BlockSpec(memory_space=pltpu.HBM)
    vmem = pl.BlockSpec(memory_space=pltpu.VMEM)
    totals = pltpu.VMEM((3, height, frames + 2, across + 2 * EDGE, outputs), f32)
    passed = pltpu.VMEM((2, height, across, outputs), bf16)
    turned = pltpu.VMEM((height, outputs, 2 * across), bf16)
    return pl.pallas_call(
        functools.partial(kernel, counts),
        out_shape=pltpu.VMEM((frames, height, across, outputs), bf16),
        in_specs=[hbm] * 9,
        out_specs=vmem,
        scratch_shapes=[
            pltpu.VMEM(b1.shape, f32),
            pltpu.VMEM(g1.shape, f32),
            pltpu.VMEM(b2.shape, f32),
            pltpu.VMEM(g2.shape, f32),
            pltpu.VMEM(bs.shape, f32),
            pltpu.VMEM(features.shape, bf16),
            pltpu.VMEM((3, 3, 3, outputs, inputs), bf16),
            pltpu.VMEM((3, 3, 3, outputs, outputs), bf16),
            pltpu.VMEM((outputs, inputs), bf16),
            pltpu.VMEM((frames, across, 2 * inputs), bf16),
            pltpu.VMEM((2, frames, across, outputs), bf16),
            pltpu.VMEM((2, frames, across, inputs), bf16),
            pltpu.VMEM((2, frames, across, outputs), bf16),
            pltpu.VMEM((height, 3, 3, outputs, frames * across), f32),
            totals,
            pltpu.VMEM((frames, height, across, outputs), f32),
            turned, turned, passed, passed,
            pltpu.SemaphoreType.DMA((11,)),
            pltpu.SemaphoreType.DMA((4, 2)),
            pltpu.SemaphoreType.DMA((4, 2)),
            pltpu.SemaphoreType.DMA((2,)),
            pltpu.SemaphoreType.DMA((2,)),
        ],
        compiler_params=pltpu.CompilerParams(
            collective_id=0, has_side_effects=True, vmem_limit_bytes=63 * 1024 * 1024
        ),
        name="block",
    )(
        features,
        jnp.swapaxes(w1, 3, 4),
        b1,
        g1,
        w2,
        b2,
        g2,
        jnp.swapaxes(ws, 0, 1),
        bs,
    )


def solution(mesh):
    counts = (mesh.shape["tm"], mesh.shape["rows"])
    return jax.shard_map(
        functools.partial(per_device, counts),
        mesh=mesh,
        in_specs=(P("tm", "rows", None, None), P(), P(), P(), P(), P(), P(), P(), P()),
        out_specs=P("tm", "rows", None, None),
        check_vma=False,
    )
```
